32 devices in a mesh: kz: 8 (over y, x, core), pw: 4 (over z).
Axes of the slice: x: 2, y: 2, z: 4, core: 2. Of those that a mesh axis runs over, the one named last changes fastest.
Arguments:
- states: bfloat16 [8, 2, 384, 512, 128], P('kz', None, None, 'pw'), may hold values from -1.25 to 1.25
- stick_perm: int32 [512], P('pw'), may hold values from 0 to 511, as said below
Outputs:
- margin: float32 [384, 8, 2, 384], P('pw', 'kz')
The draws below stay inside these ranges and needn't reach their ends.
Inputs may be any that keep to these rules, and one draw needn't show every extreme that they name: `stick_perm`: each aligned run of 128 entries, starting at a multiple of 128, is a permutation of the stick numbers of that run.
All inputs are finite; a program needn't handle non-finite values.
Results may differ from the reference program's by a relative error of at most 0.0003.
Values may be sent and summed in bfloat16 or wider, within the bound.
A program may use at most 192 MiB of HBM per device.

```python
import jax
import jax.numpy as jnp
from jax import lax

NB = 384
SL = 128
SDEV = 128
NK = 8
NSTICK = 512
NPW = 65536


def one_block(block_key):
    return jax.random.permutation(block_key, SDEV)


def draw_stick_perm(key, part):
    blocks = NSTICK // SDEV
    keys = jax.random.split(key, blocks)
    perms = jax.vmap(one_block)(keys).astype(jnp.int32)
    offsets = (jnp.arange(blocks, dtype=jnp.int32) * SDEV)[:, None]
    return (perms + offsets).reshape(NSTICK)


def raised(entries, stream_key, source, target, blocks, factor):
    def block_of(axis_at):
        return (jnp.arange(entries.shape[axis_at]) // (entries.shape[axis_at] // blocks)).reshape((-1,) + (1,) * (entries.ndim - 1 - axis_at))

    one_side = jax.random.permutation(stream_key, blocks)[block_of(target)]
    second = (block_of(target) + blocks // 2) % blocks
    return jnp.where((block_of(source) == one_side) | (block_of(source) == second), factor * entries, entries)


def levels(rng, extent, cuts, smallest, high):
    factor_of = 1.0
    for axis_at, parts in cuts:
        heights = jax.random.uniform(jax.random.fold_in(jax.random.fold_in(rng, 6), axis_at), (parts,), jnp.float32, smallest / len(cuts), high / len(cuts))
        factor_of = factor_of * jnp.repeat(jnp.exp(heights), extent[axis_at] // parts).reshape((-1,) + (1,) * (len(extent) - 1 - axis_at))
    return factor_of


def bell_draw_with(own_key, dims, width, reach, cuts, heavy, kind=jnp.bfloat16):
    array = width * jax.random.normal(own_key, dims, jnp.float32)
    if cuts:
        array = array * levels(own_key, dims, cuts, -0.22, 0.18)
    return jnp.clip(raised(array, jax.random.fold_in(own_key, 3), *heavy), -reach, reach).astype(kind)


def setup_inputs(seed: int = 0) -> dict:
    key_of = jax.random.split(jax.random.key(seed), 3)
    states = bell_draw_with(key_of[0], (NK, 2, NB, NSTICK, SL), (NPW ** -0.25), 1.25, ((0, 8), (3, 4)), (3, 2, 4, 2.0))
    stick_perm = draw_stick_perm(jax.random.fold_in(key_of[2], 71), 0)
    return dict(states=states, stick_perm=stick_perm)


def wrap_shift(state, perm):
    moved = jnp.take(state, perm, axis=2)
    return jnp.concatenate([moved[..., 1:], jnp.zeros_like(moved[..., :1])], axis=-1)


def pair_margin(left_state, right_state):
    left_flat = left_state.astype(jnp.float32).reshape(2, NB, -1)
    right_flat = right_state.astype(jnp.float32).reshape(2, NB, -1)
    products = jnp.einsum("amp,bnp->mabn", left_flat, right_flat, precision=lax.Precision.HIGHEST)
    real_part = products[:, 0, 0] + products[:, 1, 1]
    imag_part = products[:, 0, 1] - products[:, 1, 0]
    return jnp.stack([real_part, imag_part], axis=1)


def reference(states, stick_perm):
    wrapped = wrap_shift(states[0], stick_perm)

    def one_point(index):
        left_state = lax.dynamic_index_in_dim(states, index, 0, keepdims=False)
        following = lax.dynamic_index_in_dim(states, (index + 1) % NK, 0, keepdims=False)
        right_state = jnp.where(index == NK - 1, wrapped, following)
        return pair_margin(left_state, right_state)

    result = lax.map(one_point, jnp.arange(NK, dtype=jnp.int32))
    return jnp.transpose(result, (1, 0, 2, 3))
```

```python
import functools

import jax
import jax.numpy as jnp
from jax import lax
from jax.experimental import pallas as pl
from jax.experimental.pallas import tpu as pltpu
from jax.sharding import PartitionSpec as P

MESH = pl.DeviceIdType.MESH
GROUP = 16
CHUNK = 64
PIECE = 32
AHEAD = 12


def exchange_matrix():
    row = lax.broadcasted_iota(jnp.int32, (GROUP * GROUP, GROUP * GROUP), 0)
    col = lax.broadcasted_iota(jnp.int32, (GROUP * GROUP, GROUP * GROUP), 1)
    source = (row % GROUP) * GROUP + row // GROUP
    return jnp.where(col == source, 1.0, 0.0).astype(jnp.bfloat16)


def kernel(
    nk, npw, perm_ref, states_ref, out_ref,
    a_flat, a_stage, land, b_flat, acc, part, got, swap,
    load_sem, send_sem, recv_sem, part_send, part_recv,
):
    bands, sticks, length = states_ref.shape[2:]
    chunks = bands // CHUNK
    cuts = sticks // PIECE
    pieces = chunks * cuts
    depth = PIECE * length
    rows = bands // npw
    groups = 2 * bands // GROUP
    kz = lax.axis_index("kz")
    pw = lax.axis_index("pw")
    before = lax.rem(kz + nk - 1, nk)
    after = lax.rem(kz + 1, nk)

    def load(group):
        band = lax.rem(group, groups // 2) * GROUP
        return pltpu.make_async_copy(
            states_ref.at[0, group // (groups // 2), pl.ds(band, GROUP)],
            a_stage.at[lax.rem(group, 2)],
            load_sem.at[lax.rem(group, 2)],
        )

    def send(piece):
        band = (piece // cuts) * CHUNK
        stick = lax.rem(piece, cuts) * PIECE
        return pltpu.make_async_remote_copy(
            src_ref=states_ref.at[0, :, pl.ds(band, CHUNK), pl.ds(stick, PIECE)],
            dst_ref=land.at[piece],
            send_sem=send_sem.at[piece],
            recv_sem=recv_sem.at[piece],
            device_id=(before, pw),
            device_id_type=MESH,
        )

    def share(chunk, step):
        other = lax.rem(pw + step, npw)
        return pltpu.make_async_remote_copy(
            src_ref=part.at[chunk, pl.ds(pl.multiple_of(other * rows, 8), rows)],
            dst_ref=got.at[chunk, step - 1],
            send_sem=part_send.at[chunk, step - 1],
            recv_sem=part_recv.at[chunk, step - 1],
            device_id=(kz, other),
            device_id_type=MESH,
        )

    load(0).start()
    barrier = pltpu.get_barrier_semaphore()
    for neighbour in (before, after):
        pl.semaphore_signal(barrier, inc=1, device_id=(neighbour, pw), device_id_type=MESH)
    for step in range(1, npw):
        other = lax.rem(pw + step, npw)
        pl.semaphore_signal(barrier, inc=1, device_id=(kz, other), device_id_type=MESH)
    pl.semaphore_wait(barrier, npw + 1)

    @pl.loop(0, min(AHEAD, pieces))
    def _(piece):
        send(piece).start()

    swap[...] = exchange_matrix()

    def flatten(block):
        wide = [block[:, s : s + GROUP].reshape(GROUP * GROUP, length) for s in (0, GROUP)]
        moved = jnp.dot(swap[...], jnp.concatenate(wide, axis=1), preferred_element_type=jnp.float32)
        moved = moved.astype(jnp.bfloat16)
        cells = [
            moved[GROUP * s : GROUP * (s + 1), half * length : (half + 1) * length]
            for half in range(2)
            for s in range(GROUP)
        ]
        return jnp.concatenate(cells, axis=1)

    @pl.loop(0, groups)
    def _(group):
        @pl.when(group + 1 < groups)
        def _():
            load(group + 1).start()

        load(group).wait()
        slot = lax.rem(group, 2)

        @pl.when(kz == nk - 1)
        def _():
            local = perm_ref[...] - pw * sticks
            target = lax.broadcasted_iota(jnp.int32, (sticks, sticks), 0)
            place = jnp.where(target == local, 1.0, 0.0).astype(jnp.bfloat16)
            lane = lax.broadcasted_iota(jnp.int32, (sticks, length), 1)
            for band in range(GROUP):
                moved = jnp.dot(place, a_stage[slot, band], preferred_element_type=jnp.float32)
                moved = jnp.where(lane == 0, 0.0, pltpu.roll(moved, 1, 1))
                a_stage[slot, band] = moved.astype(jnp.bfloat16)

        row = pl.multiple_of(group * GROUP, GROUP)
        for cut in range(sticks // (2 * GROUP)):
            block = a_stage[slot, :, cut * 2 * GROUP : (cut + 1) * 2 * GROUP]
            a_flat[pl.ds(row, GROUP), cut * 2 * GROUP * length : (cut + 1) * 2 * GROUP * length] = flatten(block)

    @pl.loop(0, pieces)
    def _(piece):
        chunk = piece // cuts
        cut = lax.rem(piece, cuts)
        send(piece).wait_recv()
        for comp in range(2):
            for group in range(CHUNK // GROUP):
                for part_of in range(PIECE // (2 * GROUP)):
                    block = land[piece, comp, group * GROUP : (group + 1) * GROUP, part_of * 2 * GROUP : (part_of + 1) * 2 * GROUP]
                    row = comp * CHUNK + group * GROUP
                    b_flat[row : row + GROUP, part_of * 2 * GROUP * length : (part_of + 1) * 2 * GROUP * length] = flatten(block)
        at = pl.multiple_of(cut * depth, depth)
        product = lax.dot_general(
            a_flat[:, pl.ds(at, depth)], b_flat[...], (((1,), (1,)), ((), ())),
            preferred_element_type=jnp.float32,
        )

        @pl.when(cut == 0)
        def _():
            acc[...] = product

        @pl.when(cut > 0)
        def _():
            acc[...] += product

        @pl.when(cut == cuts - 1)
        def _():
            total = acc[...]
            turned = pltpu.roll(total[bands:], CHUNK, 1)
            lane = lax.broadcasted_iota(jnp.int32, (bands, 2 * CHUNK), 1)
            part[chunk] = total[:bands] + jnp.where(lane < CHUNK, turned, -turned)
            for step in range(1, npw):
                share(chunk, step).start()

        send(piece).wait_send()

        @pl.when(piece + AHEAD < pieces)
        def _():
            send(piece + AHEAD).start()

    @pl.loop(0, chunks)
    def _(chunk):
        for step in range(1, npw):
            share(chunk, step).wait()
        total = part[chunk, pl.ds(pl.multiple_of(pw * rows, 8), rows)]
        for step in range(1, npw):
            total += got[chunk, step - 1]
        out_ref[chunk] = total


def margins(nk, npw, states, stick_perm):
    _, _, bands, sticks, length = states.shape
    chunks = bands // CHUNK
    pieces = chunks * (sticks // PIECE)
    rows = bands // npw
    blocks = pl.pallas_call(
        functools.partial(kernel, nk, npw),
        out_shape=jax.ShapeDtypeStruct((chunks, rows, 2 * CHUNK), jnp.float32),
        in_specs=[pl.BlockSpec(memory_space=pltpu.VMEM), pl.BlockSpec(memory_space=pl.ANY)],
        out_specs=pl.BlockSpec(memory_space=pltpu.VMEM),
        scratch_shapes=[
            pltpu.VMEM((2 * bands, sticks * length), jnp.bfloat16),
            pltpu.VMEM((2, GROUP, sticks, length), jnp.bfloat16),
            pltpu.VMEM((pieces, 2, CHUNK, PIECE, length), jnp.bfloat16),
            pltpu.VMEM((2 * CHUNK, PIECE * length), jnp.bfloat16),
            pltpu.VMEM((2 * bands, 2 * CHUNK), jnp.float32),
            pltpu.VMEM((chunks, bands, 2 * CHUNK), jnp.float32),
            pltpu.VMEM((chunks, npw - 1, rows, 2 * CHUNK), jnp.float32),
            pltpu.VMEM((GROUP * GROUP, GROUP * GROUP), jnp.bfloat16),
            pltpu.SemaphoreType.DMA((2,)),
            pltpu.SemaphoreType.DMA((pieces,)),
            pltpu.SemaphoreType.DMA((pieces,)),
            pltpu.SemaphoreType.DMA((chunks, npw - 1)),
            pltpu.SemaphoreType.DMA((chunks, npw - 1)),
        ],
        compiler_params=pltpu.CompilerParams(
            collective_id=0, has_side_effects=True, vmem_limit_bytes=60 * 2**20
        ),
        cost_estimate=pl.CostEstimate(
            flops=8 * bands * bands * sticks * length,
            bytes_accessed=4 * states.size,
            transcendentals=0,
        ),
    )(stick_perm.reshape(1, sticks), states)
    split = blocks.reshape(chunks, rows, 2, CHUNK)
    return jnp.transpose(split, (1, 2, 0, 3)).reshape(rows, 1, 2, bands)


def solution(mesh):
    in_specs = (P("kz", None, None, "pw", None), P("pw"))
    out_specs = P("pw", "kz", None, None)
    shards = functools.partial(margins, mesh.shape["kz"], mesh.shape["pw"])
    return jax.shard_map(shards, mesh=mesh, in_specs=in_specs, out_specs=out_specs, check_vma=False)
```

```python
import functools

import jax
import jax.numpy as jnp
from jax import lax
from jax.experimental import pallas as pl
from jax.experimental.pallas import tpu as pltpu
from jax.sharding import PartitionSpec as P

MESH = pl.DeviceIdType.MESH
GROUP = 16
CHUNK = 64
PIECE = 16
AHEAD = 16


def exchange_matrix():
    row = lax.broadcasted_iota(jnp.int32, (GROUP * GROUP, GROUP * GROUP), 0)
    col = lax.broadcasted_iota(jnp.int32, (GROUP * GROUP, GROUP * GROUP), 1)
    source = (row % GROUP) * GROUP + row // GROUP
    return jnp.where(col == source, 1.0, 0.0).astype(jnp.bfloat16)


def kernel(
    nk, npw, perm_ref, states_ref, out_ref,
    a_flat, a_stage, land, b_flat, acc, part, got, swap,
    load_sem, send_sem, recv_sem, part_send, part_recv,
):
    bands, sticks, length = states_ref.shape[2:]
    chunks = bands // CHUNK
    cuts = sticks // PIECE
    pieces = chunks * cuts
    depth = PIECE * length
    rows = bands // npw
    groups = 2 * bands // GROUP
    kz = lax.axis_index("kz")
    pw = lax.axis_index("pw")
    before = lax.rem(kz + nk - 1, nk)
    after = lax.rem(kz + 1, nk)

    def load(group):
        band = lax.rem(group, groups // 2) * GROUP
        return pltpu.make_async_copy(
            states_ref.at[0, group // (groups // 2), pl.ds(band, GROUP)],
            a_stage.at[lax.rem(group, 2)],
            load_sem.at[lax.rem(group, 2)],
        )

    def send(piece):
        band = (piece // cuts) * CHUNK
        stick = lax.rem(piece, cuts) * PIECE
        return pltpu.make_async_remote_copy(
            src_ref=states_ref.at[0, :, pl.ds(band, CHUNK), pl.ds(stick, PIECE)],
            dst_ref=land.at[piece],
            send_sem=send_sem.at[piece],
            recv_sem=recv_sem.at[piece],
            device_id=(before, pw),
            device_id_type=MESH,
        )

    def share(chunk, step):
        other = lax.rem(pw + step, npw)
        return pltpu.make_async_remote_copy(
            src_ref=part.at[chunk, pl.ds(pl.multiple_of(other * rows, 8), rows)],
            dst_ref=got.at[chunk, step - 1],
            send_sem=part_send.at[chunk, step - 1],
            recv_sem=part_recv.at[chunk, step - 1],
            device_id=(kz, other),
            device_id_type=MESH,
        )

    load(0).start()
    barrier = pltpu.get_barrier_semaphore()
    for neighbour in (before, after):
        pl.semaphore_signal(barrier, inc=1, device_id=(neighbour, pw), device_id_type=MESH)
    for step in range(1, npw):
        other = lax.rem(pw + step, npw)
        pl.semaphore_signal(barrier, inc=1, device_id=(kz, other), device_id_type=MESH)
    pl.semaphore_wait(barrier, npw + 1)

    @pl.loop(0, min(AHEAD, pieces))
    def _(piece):
        send(piece).start()

    swap[...] = exchange_matrix()

    def flatten(pair):
        wide = [block.reshape(GROUP * GROUP, length) for block in pair]
        moved = jnp.dot(swap[...], jnp.concatenate(wide, axis=1), preferred_element_type=jnp.float32)
        moved = moved.astype(jnp.bfloat16)
        return [
            jnp.concatenate(
                [moved[GROUP * s : GROUP * (s + 1), half * length : (half + 1) * length] for s in range(GROUP)],
                axis=1,
            )
            for half in range(2)
        ]

    def collect(chunk):
        for step in range(1, npw):
            share(chunk, step).wait()
        total = part[chunk, pl.ds(pl.multiple_of(pw * rows, 8), rows)]
        for step in range(1, npw):
            total += got[chunk, step - 1]
        out_ref[chunk] = total

    @pl.loop(0, groups)
    def _(group):
        @pl.when(group + 1 < groups)
        def _():
            load(group + 1).start()

        load(group).wait()
        slot = lax.rem(group, 2)

        @pl.when(kz == nk - 1)
        def _():
            local = perm_ref[...] - pw * sticks
            target = lax.broadcasted_iota(jnp.int32, (sticks, sticks), 0)
            place = jnp.where(target == local, 1.0, 0.0).astype(jnp.bfloat16)
            lane = lax.broadcasted_iota(jnp.int32, (sticks, length), 1)
            for band in range(GROUP):
                moved = jnp.dot(place, a_stage[slot, band], preferred_element_type=jnp.float32)
                moved = jnp.where(lane == 0, 0.0, pltpu.roll(moved, 1, 1))
                a_stage[slot, band] = moved.astype(jnp.bfloat16)

        row = pl.multiple_of(group * GROUP, GROUP)
        for cut in range(0, sticks // GROUP, 2):
            pair = [a_stage[slot, :, at * GROUP : (at + 1) * GROUP] for at in (cut, cut + 1)]
            for at, flat in zip((cut, cut + 1), flatten(pair)):
                a_flat[pl.ds(row, GROUP), at * GROUP * length : (at + 1) * GROUP * length] = flat

    @pl.loop(0, pieces)
    def _(piece):
        chunk = piece // cuts
        cut = lax.rem(piece, cuts)

        @pl.when(piece == pieces - 1)
        def _():
            pl.loop(0, chunks - 1)(collect)

        send(piece).wait_recv()
        for comp in range(2):
            for group in range(0, CHUNK // GROUP, 2):
                pair = [land[piece, comp, at * GROUP : (at + 1) * GROUP] for at in (group, group + 1)]
                for at, flat in zip((group, group + 1), flatten(pair)):
                    row = comp * CHUNK + at * GROUP
                    b_flat[row : row + GROUP] = flat
        at = pl.multiple_of(cut * depth, depth)
        product = lax.dot_general(
            a_flat[:, pl.ds(at, depth)], b_flat[...], (((1,), (1,)), ((), ())),
            preferred_element_type=jnp.float32,
        )

        @pl.when(cut == 0)
        def _():
            acc[...] = product

        @pl.when(cut > 0)
        def _():
            acc[...] += product

        @pl.when(cut == cuts - 1)
        def _():
            total = acc[...]
            turned = pltpu.roll(total[bands:], CHUNK, 1)
            lane = lax.broadcasted_iota(jnp.int32, (bands, 2 * CHUNK), 1)
            part[chunk] = total[:bands] + jnp.where(lane < CHUNK, turned, -turned)
            for step in range(1, npw):
                share(chunk, step).start()

        send(piece).wait_send()

        @pl.when(piece + AHEAD < pieces)
        def _():
            send(piece + AHEAD).start()

    collect(chunks - 1)


def margins(nk, npw, states, stick_perm):
    _, _, bands, sticks, length = states.shape
    chunks = bands // CHUNK
    pieces = chunks * (sticks // PIECE)
    rows = bands // npw
    blocks = pl.pallas_call(
        functools.partial(kernel, nk, npw),
        out_shape=jax.ShapeDtypeStruct((chunks, rows, 2 * CHUNK), jnp.float32),
        in_specs=[pl.BlockSpec(memory_space=pltpu.VMEM), pl.BlockSpec(memory_space=pl.ANY)],
        out_specs=pl.BlockSpec(memory_space=pltpu.VMEM),
        scratch_shapes=[
            pltpu.VMEM((2 * bands, sticks * length), jnp.bfloat16),
            pltpu.VMEM((2, GROUP, sticks, length), jnp.bfloat16),
            pltpu.VMEM((pieces, 2, CHUNK, PIECE, length), jnp.bfloat16),
            pltpu.VMEM((2 * CHUNK, PIECE * length), jnp.bfloat16),
            pltpu.VMEM((2 * bands, 2 * CHUNK), jnp.float32),
            pltpu.VMEM((chunks, bands, 2 * CHUNK), jnp.float32),
            pltpu.VMEM((chunks, npw - 1, rows, 2 * CHUNK), jnp.float32),
            pltpu.VMEM((GROUP * GROUP, GROUP * GROUP), jnp.bfloat16),
            pltpu.SemaphoreType.DMA((2,)),
            pltpu.SemaphoreType.DMA((pieces,)),
            pltpu.SemaphoreType.DMA((pieces,)),
            pltpu.SemaphoreType.DMA((chunks, npw - 1)),
            pltpu.SemaphoreType.DMA((chunks, npw - 1)),
        ],
        compiler_params=pltpu.CompilerParams(
            collective_id=0, has_side_effects=True, vmem_limit_bytes=60 * 2**20
        ),
        cost_estimate=pl.CostEstimate(
            flops=8 * bands * bands * sticks * length,
            bytes_accessed=4 * states.size,
            transcendentals=0,
        ),
    )(stick_perm.reshape(1, sticks), states)
    split = blocks.reshape(chunks, rows, 2, CHUNK)
    return jnp.transpose(split, (1, 2, 0, 3)).reshape(rows, 1, 2, bands)


def solution(mesh):
    in_specs = (P("kz", None, None, "pw", None), P("pw"))
    out_specs = P("pw", "kz", None, None)
    shards = functools.partial(margins, mesh.shape["kz"], mesh.shape["pw"])
    return jax.shard_map(shards, mesh=mesh, in_specs=in_specs, out_specs=out_specs, check_vma=False)
```
